32 devices in a mesh: ctx: 4 (over y, core), tp: 2 (over x), dp: 4 (over z).
Axes of the slice: x: 2, y: 2, z: 4, core: 2. Of those that a mesh axis runs over, the one named last changes fastest.
Arguments:
- queries: bfloat16 [4, 512, 8192], P('dp', 'ctx', 'tp'), may hold values from -6 to 6
- keys: bfloat16 [4, 512, 8192], P('dp', 'ctx', 'tp'), may hold values from -6 to 6
- values: bfloat16 [4, 512, 8192], P('dp', 'ctx', 'tp'), may hold values from -6 to 6
- rates: float32 [8192, 16], P(('tp', 'dp')), may hold values from 0.0001953125 to 0.1
- residues: float32 [8192, 16], P(('tp', 'dp')), may hold values from -1.5 to 1.5
- skip: float32 [8192], P(('tp', 'dp')), may hold values from -3 to 3
Outputs:
- gated: bfloat16 [4, 512, 8192], P('dp', 'ctx', 'tp')
The draws below stay inside these ranges and needn't reach their ends.
All inputs are finite; a program needn't handle non-finite values.
Results may differ from the reference program's by a relative error of at most 0.015.
Values may be sent and summed in bfloat16 or wider, within the bound.
A program may use at most 64 MiB of HBM per device.

```python
import math
import jax
import jax.numpy as jnp
from jax import lax

D = 8192
MODES = 16
LENGTH = 512
BATCH = 4


def levels(stream_key, dims, split, least, top_value):
    loudness = 1.0
    for position, parts in split:
        heights = jax.random.uniform(jax.random.fold_in(jax.random.fold_in(stream_key, 6), position), (parts,), jnp.float32, least / len(split), top_value / len(split))
        loudness = loudness * jnp.repeat(jnp.exp(heights), dims[position] // parts).reshape((-1,) + (1,) * (len(dims) - 1 - position))
    return loudness


def normal_values(rng, shape, scale, reach, split=(), dtype=jnp.bfloat16):
    drawn = jax.random.normal(rng, shape, jnp.float32) * scale
    if len(split) > 0:
        drawn = levels(rng, shape, split, -0.22, 0.18) * drawn
    return jnp.clip(drawn, min=-reach, max=reach).astype(dtype)


def setup_inputs(seed: int = 0) -> dict:
    seeds = jax.random.split(jax.random.key(seed), 7)
    queries = normal_values(seeds[0], (BATCH, LENGTH, D), 1.0, 6.0, ((0, 4), (1, 4), (2, 2)))
    keys = normal_values(seeds[1], (BATCH, LENGTH, D), 1.0, 6.0, ((0, 4), (1, 4), (2, 2)))
    values = normal_values(seeds[2], (BATCH, LENGTH, D), 1.0, 6.0, ((0, 4), (1, 4), (2, 2)))
    rates = jnp.clip(jnp.exp(math.log(0.1) - 6.2383246 * jax.random.uniform(seeds[3], (D, MODES), jnp.float32) ** levels(seeds[3], (D, MODES), ((0, 8),), -0.2, 0.2)), 0.0001953125, 0.1)
    residues = normal_values(seeds[4], (D, MODES), 0.25, 1.5, ((0, 8),), jnp.float32)
    skip = normal_values(seeds[5], (D,), 0.5, 3.0, ((0, 8),), jnp.float32)
    return {"queries": queries, "keys": keys, "values": values, "rates": rates, "residues": residues, "skip": skip}


def convolve_group(product, decay_rates, residue_modes):
    length = product.shape[1]
    positions = jnp.arange(length).astype(jnp.float32)
    mode_gains = residue_modes * jnp.sqrt(2.0 * decay_rates)
    filter_taps = lax.optimization_barrier(jnp.sum(mode_gains[None] * jnp.exp(-decay_rates[None] * positions[:, None, None]), axis=2))
    spec_input = jnp.fft.rfft(product, n=2 * length, axis=1)
    spec_filter = jnp.fft.rfft(filter_taps, n=2 * length, axis=0)
    return jnp.fft.irfft(spec_input * spec_filter[None], n=2 * length, axis=1)[:, :length]

def reference(queries, keys, values, rates, residues, skip):
    mixed = (keys.astype(jnp.float32) * values.astype(jnp.float32)).astype(jnp.bfloat16)
    batch_size, length, channels = mixed.shape
    group_width = min(channels, 256)
    groups = channels // group_width
    product = mixed.astype(jnp.float32).reshape(batch_size, length, groups, group_width).transpose(2, 0, 1, 3)
    grouped_rates = rates.reshape(groups, group_width, rates.shape[1])
    grouped_residues = residues.reshape(groups, group_width, residues.shape[1])
    convolved = lax.map(lambda items: convolve_group(items[0], items[1], items[2]), (product, grouped_rates, grouped_residues))
    convolved = convolved.transpose(1, 2, 0, 3).reshape(batch_size, length, channels)
    gated = queries.astype(jnp.float32) * (convolved + skip[None, None, :] * mixed.astype(jnp.float32))
    return gated.astype(jnp.bfloat16)
```

```python
import functools
import math

import jax
import jax.numpy as jnp
import ml_dtypes
import numpy as np
from jax import lax
from jax.experimental import pallas as pl
from jax.experimental.pallas import tpu as pltpu
from jax.sharding import PartitionSpec as P

MESH = pl.DeviceIdType.MESH
LANES = 128


def transforms(block):
    bins = np.arange(block, dtype=np.int64)
    turns = (2 * bins[:, None] + 1) * bins[None, :] % (4 * block)
    angle = 2.0 * math.pi / (4 * block) * turns
    forward = np.concatenate([np.cos(angle), np.sin(angle)], axis=0)
    inverse = forward.T / block
    return forward.astype(ml_dtypes.bfloat16), inverse.astype(ml_dtypes.bfloat16)


def kernel(
    sizes,
    q_hbm, k_hbm, v_hbm, rates_ref, residues_ref, skip_ref, fwd_hbm, inv_hbm,
    out_hbm,
    kb, vb, mixs, mixf, qf, outb, par, skp, taps, conv, fwd, inv, statef, states, staten,
    in_sem, q_sem, mix_sem, par_send, par_recv, skp_send, skp_recv, st_send, st_recv, out_sem,
):
    tokens, half, shard, modes, ctx_size, dp_size, width = sizes
    pairs = ctx_size // 2
    half_shards = dp_size // 2
    block = 2 * tokens
    chunks = half // width
    groups = width // LANES
    ctx = lax.axis_index("ctx")
    dp = lax.axis_index("dp")
    pos = ctx // 2
    core = ctx % 2
    mate_core = 1 - core
    mate = pos * 2 + mate_core
    my_cols = pl.multiple_of(core * half, LANES)
    mate_cols = pl.multiple_of(mate_core * half, LANES)
    my_rows = pl.ds(pl.multiple_of(core * tokens, 16), tokens)
    mate_rows = pl.ds(pl.multiple_of(mate_core * tokens, 16), tokens)

    load_k = pltpu.make_async_copy(k_hbm, kb, in_sem.at[0])
    load_v = pltpu.make_async_copy(v_hbm, vb, in_sem.at[1])
    load_q = pltpu.make_async_copy(q_hbm.at[:, pl.ds(my_cols, half)], qf.at[my_rows, :], in_sem.at[2])
    load_f = pltpu.make_async_copy(fwd_hbm, fwd, in_sem.at[3])
    load_i = pltpu.make_async_copy(inv_hbm, inv, in_sem.at[4])
    load_k.start()
    load_v.start()
    load_f.start()
    load_i.start()
    load_q.start()

    barrier = pltpu.get_barrier_semaphore()
    pl.semaphore_signal(barrier, inc=1, device_id={"ctx": mate}, device_id_type=MESH)
    for step in range(1, dp_size):
        pl.semaphore_signal(
            barrier, inc=1, device_id={"dp": (dp + step) % dp_size}, device_id_type=MESH
        )
    for step in range(1, pairs):
        pl.semaphore_signal(
            barrier, inc=1, device_id={"ctx": (ctx + 2 * step) % ctx_size}, device_id_type=MESH
        )

    slot = dp % half_shards
    owns = dp // half_shards == core

    @pl.when(owns)
    def _():
        decay = rates_ref[...]
        par[slot, 0] = decay.astype(jnp.bfloat16)
        par[slot, 1] = (residues_ref[...] * jnp.sqrt(2.0 * decay)).astype(jnp.bfloat16)
        skp[slot] = skip_ref[...]

    pl.semaphore_wait(barrier, 1 + (dp_size - 1) + (pairs - 1))

    def par_copy(place, target, lane):
        return pltpu.make_async_remote_copy(
            src_ref=par.at[place], dst_ref=par.at[place], send_sem=par_send.at[lane],
            recv_sem=par_recv.at[place], device_id={"dp": target}, device_id_type=MESH,
        )

    def skp_copy(place, target, lane):
        return pltpu.make_async_remote_copy(
            src_ref=skp.at[place], dst_ref=skp.at[place], send_sem=skp_send.at[lane],
            recv_sem=skp_recv.at[place], device_id={"dp": target}, device_id_type=MESH,
        )

    @pl.when(owns)
    def _():
        for step in range(1, dp_size):
            target = (dp + step) % dp_size
            par_copy(slot, target, step - 1).start()
            skp_copy(slot, target, step - 1).start()

    send_q = pltpu.make_async_remote_copy(
        src_ref=q_hbm.at[:, pl.ds(mate_cols, half)], dst_ref=qf.at[my_rows, :],
        send_sem=q_sem.at[0], recv_sem=q_sem.at[1], device_id={"ctx": mate}, device_id_type=MESH,
    )
    send_mix = pltpu.make_async_remote_copy(
        src_ref=mixs, dst_ref=mixf.at[my_rows, :],
        send_sem=mix_sem.at[0], recv_sem=mix_sem.at[1], device_id={"ctx": mate}, device_id_type=MESH,
    )

    load_k.wait()
    load_v.wait()

    @pl.loop(0, chunks)
    def _(index):
        dst = pl.ds(pl.multiple_of(index * width, LANES), width)
        src = pl.ds(pl.multiple_of(mate_cols + index * width, LANES), width)
        mixs[:, dst] = (
            kb[:, src].astype(jnp.float32) * vb[:, src].astype(jnp.float32)
        ).astype(jnp.bfloat16)

    send_mix.start()
    send_q.start()

    @pl.loop(0, chunks)
    def _(index):
        dst = pl.ds(pl.multiple_of(index * width, LANES), width)
        src = pl.ds(pl.multiple_of(my_cols + index * width, LANES), width)
        mixf[my_rows, dst] = (
            kb[:, src].astype(jnp.float32) * vb[:, src].astype(jnp.float32)
        ).astype(jnp.bfloat16)

    for place in range(half_shards):
        source = core * half_shards + place

        @pl.when(source != dp)
        def _():
            par_copy(place, source, 0).wait_recv()
            skp_copy(place, source, 0).wait_recv()

    send_mix.wait_recv()

    shard_groups = shard // LANES
    rows8 = lax.broadcasted_iota(jnp.int32, (8, LANES), 0).astype(jnp.float32)

    def spread(row):
        return jnp.broadcast_to(row, (8, LANES))

    def group_params(group):
        place = group // shard_groups
        cols = pl.ds(pl.multiple_of(group % shard_groups * LANES, LANES), LANES)
        return (
            par[place, 0, :, cols].astype(jnp.float32),
            par[place, 1, :, cols].astype(jnp.float32),
        )

    def tree(parts):
        while len(parts) > 1:
            parts = [
                parts[i] + parts[i + 1] if i + 1 < len(parts) else parts[i]
                for i in range(0, len(parts), 2)
            ]
        return parts[0]

    def exp_sums(decay, start, store):
        ratio = jnp.exp(-8.0 * decay)
        ratios = [spread(ratio[m : m + 1]) for m in range(modes)]

        def step(index, powers):
            first = tree(list(powers))
            powers = [p * a for p, a in zip(powers, ratios)]
            second = tree(powers)
            store(pl.multiple_of(index * 16, 16), jnp.concatenate([first, second], axis=0))
            return tuple(p * a for p, a in zip(powers, ratios))

        powers = tuple(
            spread(start[m : m + 1]) * jnp.exp(-spread(decay[m : m + 1]) * rows8)
            for m in range(modes)
        )
        lax.fori_loop(0, block // 16, step, powers)

    def state_copy(index, target_pos, source_pos):
        cols = pl.ds(pl.multiple_of(index * width, LANES), width)
        return pltpu.make_async_remote_copy(
            src_ref=states.at[:, cols], dst_ref=staten.at[source_pos, :, cols],
            send_sem=st_send.at[target_pos, index], recv_sem=st_recv.at[source_pos, index],
            device_id={"ctx": target_pos * 2 + core}, device_id_type=MESH,
        )

    if pairs > 1:

        @pl.when(pos < pairs - 1)
        def _():
            @pl.loop(0, chunks)
            def _(index):
                @pl.loop(0, groups)
                def _(inner):
                    group = index * groups + inner
                    cols = pl.ds(pl.multiple_of(group * LANES, LANES), LANES)
                    decay, _ = group_params(group)
                    ratio = jnp.exp(-8.0 * decay)
                    ratios = [spread(ratio[m : m + 1]) for m in range(modes)]

                    def step(row, held):
                        both = mixf[pl.ds(pl.multiple_of(row * 16, 16), 16), cols].astype(jnp.float32)
                        held = [h * a + both[0:8] for h, a in zip(held, ratios)]
                        return tuple(h * a + both[8:16] for h, a in zip(held, ratios))

                    held = tuple(jnp.zeros((8, LANES), jnp.float32) for _ in range(modes))
                    held = lax.fori_loop(0, block // 16, step, held)
                    for m in range(modes):
                        last = held[m] * jnp.exp(-spread(decay[m : m + 1]) * (7.0 - rows8))
                        statef[m : m + 1, :] = jnp.sum(last, axis=0, keepdims=True)
                    states[:, cols] = statef[...].astype(jnp.bfloat16)

                for later in range(1, pairs):

                    @pl.when(pos < later)
                    def _():
                        state_copy(index, later, pos).start()

    load_f.wait()
    load_i.wait()

    @pl.loop(0, chunks)
    def _(index):
        @pl.loop(0, groups)
        def _(inner):
            group = index * groups + inner
            cols = pl.ds(pl.multiple_of(group * LANES, LANES), LANES)
            decay, gain = group_params(group)

            def store(row, sums):
                taps[pl.ds(row, 16), pl.ds(pl.multiple_of(inner * LANES, LANES), LANES)] = sums.astype(
                    jnp.bfloat16
                )

            exp_sums(decay, gain, store)

        cols = pl.ds(pl.multiple_of(index * width, LANES), width)
        forward = fwd[...]
        spec = jnp.dot(forward, mixf[:, cols], preferred_element_type=jnp.float32)
        filt = jnp.dot(forward, taps[...], preferred_element_type=jnp.float32)
        sr, si = spec[:block], spec[block:]
        fr, fi = filt[:block], filt[block:]
        prod_r = (sr * fr - si * fi).astype(jnp.bfloat16)
        prod_i = (sr * fi + si * fr).astype(jnp.bfloat16)
        conv[:, cols] = jnp.dot(
            inv[:, :block], prod_r, preferred_element_type=jnp.float32
        ) + jnp.dot(inv[:, block:], prod_i, preferred_element_type=jnp.float32)

    load_q.wait()
    send_q.wait_recv()

    def out_copies(index):
        cols = pl.ds(pl.multiple_of(index * width, LANES), width)
        target = pl.ds(pl.multiple_of(my_cols + index * width, LANES), width)
        local = pltpu.make_async_copy(
            outb.at[my_rows, cols], out_hbm.at[:, target], out_sem.at[0, index]
        )
        remote = pltpu.make_async_remote_copy(
            src_ref=outb.at[mate_rows, cols], dst_ref=out_hbm.at[:, target],
            send_sem=out_sem.at[1, index], recv_sem=out_sem.at[2, index],
            device_id={"ctx": mate}, device_id_type=MESH,
        )
        return local, remote

    @pl.loop(0, chunks)
    def _(index):
        for earlier in range(pairs - 1):

            @pl.when(earlier < pos)
            def _():
                state_copy(index, pos, earlier).wait_recv()

        @pl.when(pos > 0)
        def _():
            @pl.loop(0, groups)
            def _(inner):
                group = index * groups + inner
                cols = pl.ds(pl.multiple_of(group * LANES, LANES), LANES)
                decay, gain = group_params(group)
                across = jnp.exp(-float(block) * decay)
                total = jnp.zeros((modes, LANES), jnp.float32)
                for earlier in range(pairs - 1):
                    total = jnp.where(
                        earlier < pos,
                        total * across + staten[earlier, :, cols].astype(jnp.float32),
                        total,
                    )
                start = total * gain * jnp.exp(-decay)

                def store(row, sums):
                    conv[pl.ds(row, 16), cols] += sums

                exp_sums(decay, start, store)

        @pl.loop(0, groups)
        def _(inner):
            group = index * groups + inner
            cols = pl.ds(pl.multiple_of(group * LANES, LANES), LANES)
            place = group // shard_groups
            direct = skp[place, :, pl.ds(pl.multiple_of(group % shard_groups * LANES, LANES), LANES)]
            outb[:, cols] = (
                qf[:, cols].astype(jnp.float32)
                * (conv[:, cols] + direct * mixf[:, cols].astype(jnp.float32))
            ).astype(jnp.bfloat16)

        local, remote = out_copies(index)
        local.start()
        remote.start()

    @pl.when(owns)
    def _():
        for step in range(1, dp_size):
            target = (dp + step) % dp_size
            par_copy(slot, target, step - 1).wait_send()
            skp_copy(slot, target, step - 1).wait_send()

    send_q.wait_send()
    send_mix.wait_send()
    for index in range(chunks):
        for later in range(1, pairs):

            @pl.when(pos < later)
            def _():
                state_copy(index, later, pos).wait_send()

        local, remote = out_copies(index)
        local.wait()
        remote.wait()


def body(queries, keys, values, rates, residues, skip):
    tokens, channels = queries.shape[1:]
    shard, modes = rates.shape
    ctx_size = lax.axis_size("ctx")
    dp_size = lax.axis_size("dp")
    pairs = ctx_size // 2
    half = channels // 2
    block = 2 * tokens
    width = min(512, half)
    chunks = half // width
    forward, inverse = transforms(block)
    any_spec = pl.BlockSpec(memory_space=pl.ANY)
    vmem_spec = pl.BlockSpec(memory_space=pltpu.VMEM)
    bf16, f32 = jnp.bfloat16, jnp.float32
    slots = max(pairs - 1, 1)
    dma = pltpu.SemaphoreType.DMA
    sizes = (tokens, half, shard, modes, ctx_size, dp_size, width)
    gated = pl.pallas_call(
        functools.partial(kernel, sizes),
        out_shape=jax.ShapeDtypeStruct((tokens, channels), bf16),
        in_specs=[any_spec] * 3 + [vmem_spec] * 3 + [any_spec] * 2,
        out_specs=any_spec,
        scratch_shapes=[
            pltpu.VMEM((tokens, channels), bf16),
            pltpu.VMEM((tokens, channels), bf16),
            pltpu.VMEM((tokens, half), bf16),
            pltpu.VMEM((block, half), bf16),
            pltpu.VMEM((block, half), bf16),
            pltpu.VMEM((block, half), bf16),
            pltpu.VMEM((dp_size // 2, 2, modes, shard), bf16),
            pltpu.VMEM((dp_size // 2, 1, shard), f32),
            pltpu.VMEM((block, width), bf16),
            pltpu.VMEM((block, half), f32),
            pltpu.VMEM((2 * block, block), bf16),
            pltpu.VMEM((block, 2 * block), bf16),
            pltpu.VMEM((modes, LANES), f32),
            pltpu.VMEM((modes, half), bf16),
            pltpu.VMEM((slots, modes, half), bf16),
            dma((5,)),
            dma((2,)),
            dma((2,)),
            dma((dp_size - 1,)),
            dma((dp_size // 2,)),
            dma((dp_size - 1,)),
            dma((dp_size // 2,)),
            dma((pairs, chunks)),
            dma((slots, chunks)),
            dma((3, chunks)),
        ],
        compiler_params=pltpu.CompilerParams(
            collective_id=0, has_side_effects=True, vmem_limit_bytes=40 * 2**20
        ),
    )(
        queries[0], keys[0], values[0], rates.T, residues.T, skip[None, :],
        jnp.asarray(forward), jnp.asarray(inverse),
    )
    return gated[None]


def solution(mesh):
    in_specs = (
        P("dp", "ctx", "tp"),
        P("dp", "ctx", "tp"),
        P("dp", "ctx", "tp"),
        P(("tp", "dp"), None),
        P(("tp", "dp"), None),
        P(("tp", "dp")),
    )
    out_specs = P("dp", "ctx", "tp")
    return jax.shard_map(body, mesh=mesh, in_specs=in_specs, out_specs=out_specs, check_vma=False)
```

```python
import functools
import math

import jax
import jax.numpy as jnp
import ml_dtypes
import numpy as np
from jax import lax
from jax.experimental import pallas as pl
from jax.experimental.pallas import tpu as pltpu
from jax.sharding import PartitionSpec as P

MESH = pl.DeviceIdType.MESH
LANES = 128


def transforms(block):
    bins = np.arange(block, dtype=np.int64)
    turns = (2 * bins[:, None] + 1) * bins[None, :] % (4 * block)
    angle = 2.0 * math.pi / (4 * block) * turns
    forward = np.concatenate([np.cos(angle), np.sin(angle)], axis=0)
    inverse = forward.T / block
    return forward.astype(ml_dtypes.bfloat16), inverse.astype(ml_dtypes.bfloat16)


def kernel(
    sizes,
    q_hbm, k_hbm, v_hbm, rates_hbm, residues_hbm, skip_hbm, fwd_hbm, inv_hbm,
    out_hbm,
    rates_ref, residues_ref, kb, vb, mixs, mixf, qf, outb, par, skp, taps, conv, fwd, inv, statef, states, staten,
    in_sem, q_sem, mix_sem, par_send, par_recv, skp_send, skp_recv, st_send, st_recv, out_sem,
):
    tokens, half, shard, modes, ctx_size, dp_size, width = sizes
    pairs = ctx_size // 2
    half_shards = dp_size // 2
    block = 2 * tokens
    chunks = half // width
    groups = width // LANES
    ctx = lax.axis_index("ctx")
    dp = lax.axis_index("dp")
    pos = ctx // 2
    core = ctx % 2
    mate_core = 1 - core
    mate = pos * 2 + mate_core
    my_cols = pl.multiple_of(core * half, LANES)
    mate_cols = pl.multiple_of(mate_core * half, LANES)
    my_rows = pl.ds(pl.multiple_of(core * tokens, 16), tokens)
    mate_rows = pl.ds(pl.multiple_of(mate_core * tokens, 16), tokens)

    load_k = pltpu.make_async_copy(k_hbm, kb, in_sem.at[0])
    load_v = pltpu.make_async_copy(v_hbm, vb, in_sem.at[1])
    load_q = pltpu.make_async_copy(q_hbm.at[:, pl.ds(my_cols, half)], qf.at[my_rows, :], in_sem.at[2])
    load_f = pltpu.make_async_copy(fwd_hbm, fwd, in_sem.at[3])
    load_i = pltpu.make_async_copy(inv_hbm, inv, in_sem.at[4])
    slot = dp % half_shards
    owns = dp // half_shards == core
    load_r = pltpu.make_async_copy(rates_hbm, rates_ref, in_sem.at[5])
    load_g = pltpu.make_async_copy(residues_hbm, residues_ref, in_sem.at[6])
    load_s = pltpu.make_async_copy(skip_hbm, skp.at[slot], in_sem.at[7])

    @pl.when(owns)
    def _():
        load_r.start()
        load_g.start()
        load_s.start()

    load_k.start()
    load_v.start()
    load_f.start()
    load_i.start()
    load_q.start()

    barrier = pltpu.get_barrier_semaphore()
    pl.semaphore_signal(barrier, inc=1, device_id={"ctx": mate}, device_id_type=MESH)
    for step in range(1, dp_size):
        pl.semaphore_signal(
            barrier, inc=1, device_id={"dp": (dp + step) % dp_size}, device_id_type=MESH
        )
    for step in range(1, pairs):
        pl.semaphore_signal(
            barrier, inc=1, device_id={"ctx": (ctx + 2 * step) % ctx_size}, device_id_type=MESH
        )

    @pl.when(owns)
    def _():
        load_r.wait()
        load_g.wait()
        load_s.wait()
        decay = rates_ref[...]
        par[slot, 0] = decay.astype(jnp.bfloat16)
        par[slot, 1] = (residues_ref[...] * jnp.sqrt(2.0 * decay)).astype(jnp.bfloat16)

    pl.semaphore_wait(barrier, 1 + (dp_size - 1) + (pairs - 1))

    def par_copy(place, target, lane):
        return pltpu.make_async_remote_copy(
            src_ref=par.at[place], dst_ref=par.at[place], send_sem=par_send.at[lane],
            recv_sem=par_recv.at[place], device_id={"dp": target}, device_id_type=MESH,
        )

    def skp_copy(place, target, lane):
        return pltpu.make_async_remote_copy(
            src_ref=skp.at[place], dst_ref=skp.at[place], send_sem=skp_send.at[lane],
            recv_sem=skp_recv.at[place], device_id={"dp": target}, device_id_type=MESH,
        )

    @pl.when(owns)
    def _():
        for step in range(1, dp_size):
            target = (dp + step) % dp_size
            par_copy(slot, target, step - 1).start()
            skp_copy(slot, target, step - 1).start()

    send_q = pltpu.make_async_remote_copy(
        src_ref=q_hbm.at[:, pl.ds(mate_cols, half)], dst_ref=qf.at[my_rows, :],
        send_sem=q_sem.at[0], recv_sem=q_sem.at[1], device_id={"ctx": mate}, device_id_type=MESH,
    )
    send_mix = pltpu.make_async_remote_copy(
        src_ref=mixs, dst_ref=mixf.at[my_rows, :],
        send_sem=mix_sem.at[0], recv_sem=mix_sem.at[1], device_id={"ctx": mate}, device_id_type=MESH,
    )

    load_k.wait()
    load_v.wait()

    @pl.loop(0, chunks)
    def _(index):
        dst = pl.ds(pl.multiple_of(index * width, LANES), width)
        src = pl.ds(pl.multiple_of(mate_cols + index * width, LANES), width)
        mixs[:, dst] = (
            kb[:, src].astype(jnp.float32) * vb[:, src].astype(jnp.float32)
        ).astype(jnp.bfloat16)

    send_mix.start()
    send_q.start()

    @pl.loop(0, chunks)
    def _(index):
        dst = pl.ds(pl.multiple_of(index * width, LANES), width)
        src = pl.ds(pl.multiple_of(my_cols + index * width, LANES), width)
        mixf[my_rows, dst] = (
            kb[:, src].astype(jnp.float32) * vb[:, src].astype(jnp.float32)
        ).astype(jnp.bfloat16)

    for place in range(half_shards):
        source = core * half_shards + place

        @pl.when(source != dp)
        def _():
            par_copy(place, source, 0).wait_recv()
            skp_copy(place, source, 0).wait_recv()

    send_mix.wait_recv()

    shard_groups = shard // LANES
    rows8 = lax.broadcasted_iota(jnp.int32, (8, LANES), 0).astype(jnp.float32)

    def spread(row):
        return jnp.broadcast_to(row, (8, LANES))

    def group_params(group):
        place = group // shard_groups
        cols = pl.ds(pl.multiple_of(group % shard_groups * LANES, LANES), LANES)
        return (
            par[place, 0, :, cols].astype(jnp.float32),
            par[place, 1, :, cols].astype(jnp.float32),
        )

    def tree(parts):
        while len(parts) > 1:
            parts = [
                parts[i] + parts[i + 1] if i + 1 < len(parts) else parts[i]
                for i in range(0, len(parts), 2)
            ]
        return parts[0]

    def exp_sums(decay, start, store):
        ratio = jnp.exp(-8.0 * decay)
        ratios = [spread(ratio[m : m + 1]) for m in range(modes)]

        def step(index, powers):
            first = tree(list(powers))
            powers = [p * a for p, a in zip(powers, ratios)]
            second = tree(powers)
            store(pl.multiple_of(index * 16, 16), jnp.concatenate([first, second], axis=0))
            return tuple(p * a for p, a in zip(powers, ratios))

        powers = tuple(
            spread(start[m : m + 1]) * jnp.exp(-spread(decay[m : m + 1]) * rows8)
            for m in range(modes)
        )
        lax.fori_loop(0, block // 16, step, powers)

    def state_copy(index, target_pos, source_pos):
        cols = pl.ds(pl.multiple_of(index * width, LANES), width)
        return pltpu.make_async_remote_copy(
            src_ref=states.at[:, cols], dst_ref=staten.at[source_pos, :, cols],
            send_sem=st_send.at[target_pos, index], recv_sem=st_recv.at[source_pos, index],
            device_id={"ctx": target_pos * 2 + core}, device_id_type=MESH,
        )

    if pairs > 1:

        @pl.when(pos < pairs - 1)
        def _():
            @pl.loop(0, chunks)
            def _(index):
                @pl.loop(0, groups)
                def _(inner):
                    group = index * groups + inner
                    cols = pl.ds(pl.multiple_of(group * LANES, LANES), LANES)
                    decay, _ = group_params(group)
                    ratio = jnp.exp(-8.0 * decay)
                    ratios = [spread(ratio[m : m + 1]) for m in range(modes)]

                    def step(row, held):
                        both = mixf[pl.ds(pl.multiple_of(row * 16, 16), 16), cols].astype(jnp.float32)
                        held = [h * a + both[0:8] for h, a in zip(held, ratios)]
                        return tuple(h * a + both[8:16] for h, a in zip(held, ratios))

                    held = tuple(jnp.zeros((8, LANES), jnp.float32) for _ in range(modes))
                    held = lax.fori_loop(0, block // 16, step, held)
                    for m in range(modes):
                        last = held[m] * jnp.exp(-spread(decay[m : m + 1]) * (7.0 - rows8))
                        statef[m : m + 1, :] = jnp.sum(last, axis=0, keepdims=True)
                    states[:, cols] = statef[...].astype(jnp.bfloat16)

                for later in range(1, pairs):

                    @pl.when(pos < later)
                    def _():
                        state_copy(index, later, pos).start()

    load_f.wait()
    load_i.wait()

    @pl.loop(0, chunks)
    def _(index):
        @pl.loop(0, groups)
        def _(inner):
            group = index * groups + inner
            cols = pl.ds(pl.multiple_of(group * LANES, LANES), LANES)
            decay, gain = group_params(group)

            def store(row, sums):
                taps[pl.ds(row, 16), pl.ds(pl.multiple_of(inner * LANES, LANES), LANES)] = sums.astype(
                    jnp.bfloat16
                )

            exp_sums(decay, gain, store)

        cols = pl.ds(pl.multiple_of(index * width, LANES), width)
        forward = fwd[...]
        spec = jnp.dot(forward, mixf[:, cols], preferred_element_type=jnp.float32)
        filt = jnp.dot(forward, taps[...], preferred_element_type=jnp.float32)
        sr, si = spec[:block], spec[block:]
        fr, fi = filt[:block], filt[block:]
        prod_r = (sr * fr - si * fi).astype(jnp.bfloat16)
        prod_i = (sr * fi + si * fr).astype(jnp.bfloat16)
        conv[:, cols] = jnp.dot(
            inv[:, :block], prod_r, preferred_element_type=jnp.float32
        ) + jnp.dot(inv[:, block:], prod_i, preferred_element_type=jnp.float32)

    load_q.wait()
    send_q.wait_recv()

    def out_copies(index):
        cols = pl.ds(pl.multiple_of(index * width, LANES), width)
        target = pl.ds(pl.multiple_of(my_cols + index * width, LANES), width)
        local = pltpu.make_async_copy(
            outb.at[my_rows, cols], out_hbm.at[:, target], out_sem.at[0, index]
        )
        remote = pltpu.make_async_remote_copy(
            src_ref=outb.at[mate_rows, cols], dst_ref=out_hbm.at[:, target],
            send_sem=out_sem.at[1, index], recv_sem=out_sem.at[2, index],
            device_id={"ctx": mate}, device_id_type=MESH,
        )
        return local, remote

    @pl.loop(0, chunks)
    def _(index):
        for earlier in range(pairs - 1):

            @pl.when(earlier < pos)
            def _():
                state_copy(index, pos, earlier).wait_recv()

        @pl.when(pos > 0)
        def _():
            @pl.loop(0, groups)
            def _(inner):
                group = index * groups + inner
                cols = pl.ds(pl.multiple_of(group * LANES, LANES), LANES)
                decay, gain = group_params(group)
                across = jnp.exp(-float(block) * decay)
                total = jnp.zeros((modes, LANES), jnp.float32)
                for earlier in range(pairs - 1):
                    total = jnp.where(
                        earlier < pos,
                        total * across + staten[earlier, :, cols].astype(jnp.float32),
                        total,
                    )
                start = total * gain * jnp.exp(-decay)

                def store(row, sums):
                    conv[pl.ds(row, 16), cols] += sums

                exp_sums(decay, start, store)

        @pl.loop(0, groups)
        def _(inner):
            group = index * groups + inner
            cols = pl.ds(pl.multiple_of(group * LANES, LANES), LANES)
            place = group // shard_groups
            direct = skp[place, :, pl.ds(pl.multiple_of(group % shard_groups * LANES, LANES), LANES)]
            outb[:, cols] = (
                qf[:, cols].astype(jnp.float32)
                * (conv[:, cols] + direct * mixf[:, cols].astype(jnp.float32))
            ).astype(jnp.bfloat16)

        local, remote = out_copies(index)
        local.start()
        remote.start()

    @pl.when(owns)
    def _():
        for step in range(1, dp_size):
            target = (dp + step) % dp_size
            par_copy(slot, target, step - 1).wait_send()
            skp_copy(slot, target, step - 1).wait_send()

    send_q.wait_send()
    send_mix.wait_send()
    for index in range(chunks):
        for later in range(1, pairs):

            @pl.when(pos < later)
            def _():
                state_copy(index, later, pos).wait_send()

        local, remote = out_copies(index)
        local.wait()
        remote.wait()


def body(queries, keys, values, rates, residues, skip):
    tokens, channels = queries.shape[1:]
    shard, modes = rates.shape
    ctx_size = lax.axis_size("ctx")
    dp_size = lax.axis_size("dp")
    pairs = ctx_size // 2
    half = channels // 2
    block = 2 * tokens
    width = min(512, half)
    chunks = half // width
    forward, inverse = transforms(block)
    hbm_spec = pl.BlockSpec(memory_space=pltpu.HBM)
    bf16, f32 = jnp.bfloat16, jnp.float32
    slots = max(pairs - 1, 1)
    dma = pltpu.SemaphoreType.DMA
    sizes = (tokens, half, shard, modes, ctx_size, dp_size, width)
    gated = pl.pallas_call(
        functools.partial(kernel, sizes),
        out_shape=jax.ShapeDtypeStruct((tokens, channels), bf16),
        in_specs=[hbm_spec] * 8,
        out_specs=hbm_spec,
        scratch_shapes=[
            pltpu.VMEM((modes, shard), f32),
            pltpu.VMEM((modes, shard), f32),
            pltpu.VMEM((tokens, channels), bf16),
            pltpu.VMEM((tokens, channels), bf16),
            pltpu.VMEM((tokens, half), bf16),
            pltpu.VMEM((block, half), bf16),
            pltpu.VMEM((block, half), bf16),
            pltpu.VMEM((block, half), bf16),
            pltpu.VMEM((dp_size // 2, 2, modes, shard), bf16),
            pltpu.VMEM((dp_size // 2, 1, shard), f32),
            pltpu.VMEM((block, width), bf16),
            pltpu.VMEM((block, half), f32),
            pltpu.VMEM((2 * block, block), bf16),
            pltpu.VMEM((block, 2 * block), bf16),
            pltpu.VMEM((modes, LANES), f32),
            pltpu.VMEM((modes, half), bf16),
            pltpu.VMEM((slots, modes, half), bf16),
            dma((8,)),
            dma((2,)),
            dma((2,)),
            dma((dp_size - 1,)),
            dma((dp_size // 2,)),
            dma((dp_size - 1,)),
            dma((dp_size // 2,)),
            dma((pairs, chunks)),
            dma((slots, chunks)),
            dma((3, chunks)),
        ],
        compiler_params=pltpu.CompilerParams(
            collective_id=0, has_side_effects=True, vmem_limit_bytes=60 * 2**20
        ),
    )(
        queries[0], keys[0], values[0], rates.T, residues.T, skip[None, :],
        jnp.asarray(forward), jnp.asarray(inverse),
    )
    return gated[None]


def solution(mesh):
    in_specs = (
        P("dp", "ctx", "tp"),
        P("dp", "ctx", "tp"),
        P("dp", "ctx", "tp"),
        P(("tp", "dp"), None),
        P(("tp", "dp"), None),
        P(("tp", "dp")),
    )
    out_specs = P("dp", "ctx", "tp")
    return jax.shard_map(body, mesh=mesh, in_specs=in_specs, out_specs=out_specs, check_vma=False)
```

```python
import functools
import math

import jax
import jax.numpy as jnp
import ml_dtypes
import numpy as np
from jax import lax
from jax.experimental import pallas as pl
from jax.experimental.pallas import tpu as pltpu
from jax.sharding import PartitionSpec as P

MESH = pl.DeviceIdType.MESH
LANES = 128
UNROLL = 16


def transforms(block):
    bins = np.arange(block, dtype=np.int64)
    turns = (2 * bins[:, None] + 1) * bins[None, :] % (4 * block)
    angle = 2.0 * math.pi / (4 * block) * turns
    forward = np.concatenate([np.cos(angle), np.sin(angle)], axis=0)
    inverse = forward.T / block
    return forward.astype(ml_dtypes.bfloat16), inverse.astype(ml_dtypes.bfloat16)


def kernel(
    sizes,
    k_hbm, v_hbm, rates_hbm, residues_hbm, skip_hbm, fwd_hbm, inv_hbm,
    out_hbm,
    rates_ref, residues_ref, kb, vb, mixs, mixf, outb, par, skp, taps, spec, conv, fwd, inv, statef, states, staten,
    in_sem, mix_sem, par_send, par_recv, skp_send, skp_recv, st_send, st_recv, out_sem,
):
    tokens, half, shard, modes, ctx_size, dp_size, width = sizes
    pairs = ctx_size // 2
    half_shards = dp_size // 2
    block = 2 * tokens
    chunks = half // width
    groups = width // LANES
    ctx = lax.axis_index("ctx")
    dp = lax.axis_index("dp")
    pos = ctx // 2
    core = ctx % 2
    mate_core = 1 - core
    mate = pos * 2 + mate_core
    my_cols = pl.multiple_of(core * half, LANES)
    mate_cols = pl.multiple_of(mate_core * half, LANES)
    my_rows = pl.ds(pl.multiple_of(core * tokens, 16), tokens)
    mate_rows = pl.ds(pl.multiple_of(mate_core * tokens, 16), tokens)

    load_k = pltpu.make_async_copy(k_hbm, kb, in_sem.at[0])
    load_v = pltpu.make_async_copy(v_hbm, vb, in_sem.at[1])
    load_f = pltpu.make_async_copy(fwd_hbm, fwd, in_sem.at[3])
    load_i = pltpu.make_async_copy(inv_hbm, inv, in_sem.at[4])
    slot = dp % half_shards
    owns = dp // half_shards == core
    load_r = pltpu.make_async_copy(rates_hbm, rates_ref, in_sem.at[5])
    load_g = pltpu.make_async_copy(residues_hbm, residues_ref, in_sem.at[6])
    load_s = pltpu.make_async_copy(skip_hbm, skp.at[slot], in_sem.at[7])

    @pl.when(owns)
    def _():
        load_r.start()
        load_g.start()
        load_s.start()

    load_k.start()
    load_v.start()
    load_f.start()
    load_i.start()

    barrier = pltpu.get_barrier_semaphore()
    pl.semaphore_signal(barrier, inc=1, device_id={"ctx": mate}, device_id_type=MESH)
    for step in range(1, dp_size):
        pl.semaphore_signal(
            barrier, inc=1, device_id={"dp": (dp + step) % dp_size}, device_id_type=MESH
        )
    for step in range(1, pairs):
        pl.semaphore_signal(
            barrier, inc=1, device_id={"ctx": (ctx + 2 * step) % ctx_size}, device_id_type=MESH
        )

    @pl.when(owns)
    def _():
        load_r.wait()
        load_g.wait()
        load_s.wait()
        decay = rates_ref[...]
        par[slot, 0] = decay.astype(jnp.bfloat16)
        par[slot, 1] = (residues_ref[...] * jnp.sqrt(2.0 * decay)).astype(jnp.bfloat16)

    pl.semaphore_wait(barrier, 1 + (dp_size - 1) + (pairs - 1))

    def par_copy(place, target, lane):
        return pltpu.make_async_remote_copy(
            src_ref=par.at[place], dst_ref=par.at[place], send_sem=par_send.at[lane],
            recv_sem=par_recv.at[place], device_id={"dp": target}, device_id_type=MESH,
        )

    def skp_copy(place, target, lane):
        return pltpu.make_async_remote_copy(
            src_ref=skp.at[place], dst_ref=skp.at[place], send_sem=skp_send.at[lane],
            recv_sem=skp_recv.at[place], device_id={"dp": target}, device_id_type=MESH,
        )

    @pl.when(owns)
    def _():
        for step in range(1, dp_size):
            target = (dp + step) % dp_size
            par_copy(slot, target, step - 1).start()
            skp_copy(slot, target, step - 1).start()

    send_mix = pltpu.make_async_remote_copy(
        src_ref=mixs, dst_ref=mixf.at[my_rows, :],
        send_sem=mix_sem.at[0], recv_sem=mix_sem.at[1], device_id={"ctx": mate}, device_id_type=MESH,
    )

    load_k.wait()
    load_v.wait()

    @pl.loop(0, chunks)
    def _(index):
        dst = pl.ds(pl.multiple_of(index * width, LANES), width)
        src = pl.ds(pl.multiple_of(mate_cols + index * width, LANES), width)
        mixs[:, dst] = (
            kb[:, src].astype(jnp.float32) * vb[:, src].astype(jnp.float32)
        ).astype(jnp.bfloat16)

    send_mix.start()

    @pl.loop(0, chunks)
    def _(index):
        dst = pl.ds(pl.multiple_of(index * width, LANES), width)
        src = pl.ds(pl.multiple_of(my_cols + index * width, LANES), width)
        mixf[my_rows, dst] = (
            kb[:, src].astype(jnp.float32) * vb[:, src].astype(jnp.float32)
        ).astype(jnp.bfloat16)

    load_f.wait()
    load_i.wait()
    send_mix.wait_recv()

    @pl.loop(0, chunks)
    def _(index):
        cols = pl.ds(pl.multiple_of(index * width, LANES), width)
        spec[:, cols] = jnp.dot(fwd[...], mixf[:, cols], preferred_element_type=jnp.float32)

    for place in range(half_shards):
        source = core * half_shards + place

        @pl.when(source != dp)
        def _():
            par_copy(place, source, 0).wait_recv()
            skp_copy(place, source, 0).wait_recv()

    shard_groups = shard // LANES
    rows8 = lax.broadcasted_iota(jnp.int32, (8, LANES), 0).astype(jnp.float32)

    def spread(row):
        return jnp.broadcast_to(row, (8, LANES))

    def group_params(group):
        place = group // shard_groups
        cols = pl.ds(pl.multiple_of(group % shard_groups * LANES, LANES), LANES)
        return (
            par[place, 0, :, cols].astype(jnp.float32),
            par[place, 1, :, cols].astype(jnp.float32),
        )

    def tree(parts):
        while len(parts) > 1:
            parts = [
                parts[i] + parts[i + 1] if i + 1 < len(parts) else parts[i]
                for i in range(0, len(parts), 2)
            ]
        return parts[0]

    def exp_sums(decay, start, store):
        ratio = jnp.exp(-8.0 * decay)
        ratios = [spread(ratio[m : m + 1]) for m in range(modes)]

        def step(index, powers):
            first = tree(list(powers))
            powers = [p * a for p, a in zip(powers, ratios)]
            second = tree(powers)
            store(pl.multiple_of(index * 16, 16), jnp.concatenate([first, second], axis=0))
            return tuple(p * a for p, a in zip(powers, ratios))

        powers = tuple(
            spread(start[m : m + 1]) * jnp.exp(-spread(decay[m : m + 1]) * rows8)
            for m in range(modes)
        )
        lax.fori_loop(0, block // 16, step, powers, unroll=UNROLL)

    def state_copy(index, target_pos, source_pos):
        cols = pl.ds(pl.multiple_of(index * width, LANES), width)
        return pltpu.make_async_remote_copy(
            src_ref=states.at[:, cols], dst_ref=staten.at[source_pos, :, cols],
            send_sem=st_send.at[target_pos, index], recv_sem=st_recv.at[source_pos, index],
            device_id={"ctx": target_pos * 2 + core}, device_id_type=MESH,
        )

    if pairs > 1:

        @pl.when(pos < pairs - 1)
        def _():
            @pl.loop(0, chunks)
            def _(index):
                @pl.loop(0, groups)
                def _(inner):
                    group = index * groups + inner
                    cols = pl.ds(pl.multiple_of(group * LANES, LANES), LANES)
                    decay, _ = group_params(group)
                    ratio = jnp.exp(-8.0 * decay)
                    ratios = [spread(ratio[m : m + 1]) for m in range(modes)]

                    def step(row, held):
                        both = mixf[pl.ds(pl.multiple_of(row * 16, 16), 16), cols].astype(jnp.float32)
                        held = [h * a + both[0:8] for h, a in zip(held, ratios)]
                        return tuple(h * a + both[8:16] for h, a in zip(held, ratios))

                    held = tuple(jnp.zeros((8, LANES), jnp.float32) for _ in range(modes))
                    held = lax.fori_loop(0, block // 16, step, held, unroll=UNROLL)
                    for m in range(modes):
                        last = held[m] * jnp.exp(-spread(decay[m : m + 1]) * (7.0 - rows8))
                        statef[m : m + 1, :] = jnp.sum(last, axis=0, keepdims=True)
                    states[:, cols] = statef[...].astype(jnp.bfloat16)

                for later in range(1, pairs):

                    @pl.when(pos < later)
                    def _():
                        state_copy(index, later, pos).start()

    @pl.loop(0, chunks)
    def _(index):
        @pl.loop(0, groups)
        def _(inner):
            group = index * groups + inner
            cols = pl.ds(pl.multiple_of(group * LANES, LANES), LANES)
            decay, gain = group_params(group)

            def store(row, sums):
                taps[pl.ds(row, 16), pl.ds(pl.multiple_of(inner * LANES, LANES), LANES)] = sums.astype(
                    jnp.bfloat16
                )

            exp_sums(decay, gain, store)

        cols = pl.ds(pl.multiple_of(index * width, LANES), width)
        filt = jnp.dot(fwd[...], taps[...], preferred_element_type=jnp.float32)
        sr, si = spec[:block, cols], spec[block:, cols]
        fr, fi = filt[:block], filt[block:]
        prod_r = (sr * fr - si * fi).astype(jnp.bfloat16)
        prod_i = (sr * fi + si * fr).astype(jnp.bfloat16)
        conv[:, cols] = jnp.dot(
            inv[:, :block], prod_r, preferred_element_type=jnp.float32
        ) + jnp.dot(inv[:, block:], prod_i, preferred_element_type=jnp.float32)

    def out_copies(index):
        cols = pl.ds(pl.multiple_of(index * width, LANES), width)
        target = pl.ds(pl.multiple_of(my_cols + index * width, LANES), width)
        local = pltpu.make_async_copy(
            outb.at[my_rows, cols], out_hbm.at[:, target], out_sem.at[0, index]
        )
        remote = pltpu.make_async_remote_copy(
            src_ref=outb.at[mate_rows, cols], dst_ref=out_hbm.at[:, target],
            send_sem=out_sem.at[1, index], recv_sem=out_sem.at[2, index],
            device_id={"ctx": mate}, device_id_type=MESH,
        )
        return local, remote

    @pl.loop(0, chunks)
    def _(index):
        for earlier in range(pairs - 1):

            @pl.when(earlier < pos)
            def _():
                state_copy(index, pos, earlier).wait_recv()

        @pl.when(pos > 0)
        def _():
            @pl.loop(0, groups)
            def _(inner):
                group = index * groups + inner
                cols = pl.ds(pl.multiple_of(group * LANES, LANES), LANES)
                decay, gain = group_params(group)
                across = jnp.exp(-float(block) * decay)
                total = jnp.zeros((modes, LANES), jnp.float32)
                for earlier in range(pairs - 1):
                    total = jnp.where(
                        earlier < pos,
                        total * across + staten[earlier, :, cols].astype(jnp.float32),
                        total,
                    )
                start = total * gain * jnp.exp(-decay)

                def store(row, sums):
                    conv[pl.ds(row, 16), cols] += sums

                exp_sums(decay, start, store)

        @pl.loop(0, groups)
        def _(inner):
            group = index * groups + inner
            cols = pl.ds(pl.multiple_of(group * LANES, LANES), LANES)
            place = group // shard_groups
            direct = skp[place, :, pl.ds(pl.multiple_of(group % shard_groups * LANES, LANES), LANES)]
            outb[:, cols] = (conv[:, cols] + direct * mixf[:, cols].astype(jnp.float32)).astype(
                jnp.bfloat16
            )

        local, remote = out_copies(index)
        local.start()
        remote.start()

    @pl.when(owns)
    def _():
        for step in range(1, dp_size):
            target = (dp + step) % dp_size
            par_copy(slot, target, step - 1).wait_send()
            skp_copy(slot, target, step - 1).wait_send()

    send_mix.wait_send()
    for index in range(chunks):
        for later in range(1, pairs):

            @pl.when(pos < later)
            def _():
                state_copy(index, later, pos).wait_send()

        local, remote = out_copies(index)
        local.wait()
        remote.wait()


def body(queries, keys, values, rates, residues, skip):
    tokens, channels = queries.shape[1:]
    shard, modes = rates.shape
    ctx_size = lax.axis_size("ctx")
    dp_size = lax.axis_size("dp")
    pairs = ctx_size // 2
    half = channels // 2
    block = 2 * tokens
    width = min(512, half)
    chunks = half // width
    forward, inverse = transforms(block)
    hbm_spec = pl.BlockSpec(memory_space=pltpu.HBM)
    bf16, f32 = jnp.bfloat16, jnp.float32
    slots = max(pairs - 1, 1)
    dma = pltpu.SemaphoreType.DMA
    sizes = (tokens, half, shard, modes, ctx_size, dp_size, width)
    mixed_out = pl.pallas_call(
        functools.partial(kernel, sizes),
        out_shape=jax.ShapeDtypeStruct((tokens, channels), bf16),
        in_specs=[hbm_spec] * 7,
        out_specs=hbm_spec,
        scratch_shapes=[
            pltpu.VMEM((modes, shard), f32),
            pltpu.VMEM((modes, shard), f32),
            pltpu.VMEM((tokens, channels), bf16),
            pltpu.VMEM((tokens, channels), bf16),
            pltpu.VMEM((tokens, half), bf16),
            pltpu.VMEM((block, half), bf16),
            pltpu.VMEM((block, half), bf16),
            pltpu.VMEM((dp_size // 2, 2, modes, shard), bf16),
            pltpu.VMEM((dp_size // 2, 1, shard), f32),
            pltpu.VMEM((block, width), bf16),
            pltpu.VMEM((2 * block, half), f32),
            pltpu.VMEM((block, half), f32),
            pltpu.VMEM((2 * block, block), bf16),
            pltpu.VMEM((block, 2 * block), bf16),
            pltpu.VMEM((modes, LANES), f32),
            pltpu.VMEM((modes, half), bf16),
            pltpu.VMEM((slots, modes, half), bf16),
            dma((8,)),
            dma((2,)),
            dma((dp_size - 1,)),
            dma((dp_size // 2,)),
            dma((dp_size - 1,)),
            dma((dp_size // 2,)),
            dma((pairs, chunks)),
            dma((slots, chunks)),
            dma((3, chunks)),
        ],
        compiler_params=pltpu.CompilerParams(
            collective_id=0, has_side_effects=True, vmem_limit_bytes=60 * 2**20
        ),
    )(
        keys[0], values[0], rates.T, residues.T, skip[None, :],
        jnp.asarray(forward), jnp.asarray(inverse),
    )
    return (queries.astype(f32) * mixed_out[None].astype(f32)).astype(bf16)


def solution(mesh):
    in_specs = (
        P("dp", "ctx", "tp"),
        P("dp", "ctx", "tp"),
        P("dp", "ctx", "tp"),
        P(("tp", "dp"), None),
        P(("tp", "dp"), None),
        P(("tp", "dp")),
    )
    out_specs = P("dp", "ctx", "tp")
    return jax.shard_map(body, mesh=mesh, in_specs=in_specs, out_specs=out_specs, check_vma=False)
```

```python
import functools
import math

import jax
import jax.numpy as jnp
import ml_dtypes
import numpy as np
from jax import lax
from jax.experimental import pallas as pl
from jax.experimental.pallas import tpu as pltpu
from jax.sharding import PartitionSpec as P

MESH = pl.DeviceIdType.MESH
LANES = 128
UNROLL = 16


def transforms(block):
    bins = np.arange(block, dtype=np.int64)
    turns = (2 * bins[:, None] + 1) * bins[None, :] % (4 * block)
    angle = 2.0 * math.pi / (4 * block) * turns
    forward = np.concatenate([np.cos(angle), np.sin(angle)], axis=0)
    inverse = forward.T / block
    return forward.astype(ml_dtypes.bfloat16), inverse.astype(ml_dtypes.bfloat16)


def kernel(
    sizes,
    k_hbm, v_hbm, rates_hbm, residues_hbm, skip_hbm, fwd_hbm, inv_hbm,
    out_hbm,
    rates_ref, residues_ref, kb, vb, mixs, mixf, outb, par, skp, taps, spec, conv, fwd, inv, statef, states, staten,
    in_sem, mix_sem, par_send, par_recv, skp_send, skp_recv, st_send, st_recv, out_sem,
):
    tokens, half, shard, modes, ctx_size, dp_size, width = sizes
    pairs = ctx_size // 2
    half_shards = dp_size // 2
    block = 2 * tokens
    chunks = half // width
    groups = width // LANES
    ctx = lax.axis_index("ctx")
    dp = lax.axis_index("dp")
    pos = ctx // 2
    core = ctx % 2
    mate_core = 1 - core
    mate = pos * 2 + mate_core
    my_cols = pl.multiple_of(core * half, LANES)
    mate_cols = pl.multiple_of(mate_core * half, LANES)
    my_rows = pl.ds(pl.multiple_of(core * tokens, 16), tokens)
    mate_rows = pl.ds(pl.multiple_of(mate_core * tokens, 16), tokens)

    load_k = pltpu.make_async_copy(k_hbm, kb, in_sem.at[0])
    load_v = pltpu.make_async_copy(v_hbm, vb, in_sem.at[1])
    load_f = pltpu.make_async_copy(fwd_hbm, fwd, in_sem.at[3])
    load_i = pltpu.make_async_copy(inv_hbm, inv, in_sem.at[4])
    slot = dp % half_shards
    owns = dp // half_shards == core
    load_r = pltpu.make_async_copy(rates_hbm, rates_ref, in_sem.at[5])
    load_g = pltpu.make_async_copy(residues_hbm, residues_ref, in_sem.at[6])
    load_s = pltpu.make_async_copy(skip_hbm, skp.at[slot], in_sem.at[7])

    @pl.when(owns)
    def _():
        load_r.start()
        load_g.start()
        load_s.start()

    load_k.start()
    load_v.start()
    load_f.start()
    load_i.start()

    barrier = pltpu.get_barrier_semaphore()
    pl.semaphore_signal(barrier, inc=1, device_id={"ctx": mate}, device_id_type=MESH)
    for step in range(1, dp_size):
        pl.semaphore_signal(
            barrier, inc=1, device_id={"dp": (dp + step) % dp_size}, device_id_type=MESH
        )
    for step in range(1, pairs):
        pl.semaphore_signal(
            barrier, inc=1, device_id={"ctx": (ctx + 2 * step) % ctx_size}, device_id_type=MESH
        )

    @pl.when(owns)
    def _():
        load_r.wait()
        load_g.wait()
        load_s.wait()
        decay = rates_ref[...]
        par[slot, 0] = decay.astype(jnp.bfloat16)
        par[slot, 1] = (residues_ref[...] * jnp.sqrt(2.0 * decay)).astype(jnp.bfloat16)

    pl.semaphore_wait(barrier, 1 + (dp_size - 1) + (pairs - 1))

    def par_copy(place, target, lane):
        return pltpu.make_async_remote_copy(
            src_ref=par.at[place], dst_ref=par.at[place], send_sem=par_send.at[lane],
            recv_sem=par_recv.at[place], device_id={"dp": target}, device_id_type=MESH,
        )

    def skp_copy(place, target, lane):
        return pltpu.make_async_remote_copy(
            src_ref=skp.at[place], dst_ref=skp.at[place], send_sem=skp_send.at[lane],
            recv_sem=skp_recv.at[place], device_id={"dp": target}, device_id_type=MESH,
        )

    @pl.when(owns)
    def _():
        for step in range(1, dp_size):
            target = (dp + step) % dp_size
            par_copy(slot, target, step - 1).start()
            skp_copy(slot, target, step - 1).start()

    send_mix = pltpu.make_async_remote_copy(
        src_ref=mixs, dst_ref=mixf.at[my_rows, :],
        send_sem=mix_sem.at[0], recv_sem=mix_sem.at[1], device_id={"ctx": mate}, device_id_type=MESH,
    )

    load_k.wait()
    load_v.wait()

    @pl.loop(0, chunks)
    def _(index):
        dst = pl.ds(pl.multiple_of(index * width, LANES), width)
        src = pl.ds(pl.multiple_of(mate_cols + index * width, LANES), width)
        mixs[:, dst] = (
            kb[:, src].astype(jnp.float32) * vb[:, src].astype(jnp.float32)
        ).astype(jnp.bfloat16)

    send_mix.start()

    @pl.loop(0, chunks)
    def _(index):
        dst = pl.ds(pl.multiple_of(index * width, LANES), width)
        src = pl.ds(pl.multiple_of(my_cols + index * width, LANES), width)
        mixf[my_rows, dst] = (
            kb[:, src].astype(jnp.float32) * vb[:, src].astype(jnp.float32)
        ).astype(jnp.bfloat16)

    load_f.wait()
    load_i.wait()
    send_mix.wait_recv()

    @pl.loop(0, chunks)
    def _(index):
        cols = pl.ds(pl.multiple_of(index * width, LANES), width)
        spec[:, cols] = jnp.dot(fwd[...], mixf[:, cols], preferred_element_type=jnp.float32)

    for place in range(half_shards):
        source = core * half_shards + place

        @pl.when(source != dp)
        def _():
            par_copy(place, source, 0).wait_recv()
            skp_copy(place, source, 0).wait_recv()

    shard_groups = shard // LANES
    rows8 = lax.broadcasted_iota(jnp.int32, (8, LANES), 0).astype(jnp.float32)

    def spread(row):
        return jnp.broadcast_to(row, (8, LANES))

    def group_params(group):
        place = group // shard_groups
        cols = pl.ds(pl.multiple_of(group % shard_groups * LANES, LANES), LANES)
        return (
            par[place, 0, :, cols].astype(jnp.float32),
            par[place, 1, :, cols].astype(jnp.float32),
        )

    def group_skip(group):
        cols = pl.ds(pl.multiple_of(group % shard_groups * LANES, LANES), LANES)
        return skp[group // shard_groups, :, cols]

    def tree(parts):
        while len(parts) > 1:
            parts = [
                parts[i] + parts[i + 1] if i + 1 < len(parts) else parts[i]
                for i in range(0, len(parts), 2)
            ]
        return parts[0]

    def exp_sums(decay, start, store):
        ratio = jnp.exp(-8.0 * decay)
        ratios = [spread(ratio[m : m + 1]) for m in range(modes)]

        def step(index, powers):
            first = tree(list(powers))
            powers = [p * a for p, a in zip(powers, ratios)]
            second = tree(powers)
            store(pl.multiple_of(index * 16, 16), jnp.concatenate([first, second], axis=0))
            return tuple(p * a for p, a in zip(powers, ratios))

        powers = tuple(
            spread(start[m : m + 1]) * jnp.exp(-spread(decay[m : m + 1]) * rows8)
            for m in range(modes)
        )
        lax.fori_loop(0, block // 16, step, powers, unroll=UNROLL)

    def state_copy(index, target_pos, source_pos):
        cols = pl.ds(pl.multiple_of(index * width, LANES), width)
        return pltpu.make_async_remote_copy(
            src_ref=states.at[:, cols], dst_ref=staten.at[source_pos, :, cols],
            send_sem=st_send.at[target_pos, index], recv_sem=st_recv.at[source_pos, index],
            device_id={"ctx": target_pos * 2 + core}, device_id_type=MESH,
        )

    if pairs > 1:

        @pl.when(pos < pairs - 1)
        def _():
            @pl.loop(0, chunks)
            def _(index):
                @pl.loop(0, groups, unroll=True)
                def _(inner):
                    group = index * groups + inner
                    cols = pl.ds(pl.multiple_of(group * LANES, LANES), LANES)
                    decay, _ = group_params(group)
                    ratio = jnp.exp(-8.0 * decay)
                    ratios = [spread(ratio[m : m + 1]) for m in range(modes)]

                    def step(row, held):
                        both = mixf[pl.ds(pl.multiple_of(row * 16, 16), 16), cols].astype(jnp.float32)
                        held = [h * a + both[0:8] for h, a in zip(held, ratios)]
                        return tuple(h * a + both[8:16] for h, a in zip(held, ratios))

                    held = tuple(jnp.zeros((8, LANES), jnp.float32) for _ in range(modes))
                    held = lax.fori_loop(0, block // 16, step, held, unroll=UNROLL)
                    for m in range(modes):
                        last = held[m] * jnp.exp(-spread(decay[m : m + 1]) * (7.0 - rows8))
                        statef[m : m + 1, :] = jnp.sum(last, axis=0, keepdims=True)
                    states[:, cols] = statef[...].astype(jnp.bfloat16)

                for later in range(1, pairs):

                    @pl.when(pos < later)
                    def _():
                        state_copy(index, later, pos).start()

    def make_taps(index):
        for inner in range(groups):
            decay, gain = group_params(index * groups + inner)

            def store(row, sums):
                taps[index, pl.ds(row, 16), inner * LANES : (inner + 1) * LANES] = sums.astype(
                    jnp.bfloat16
                )

            exp_sums(decay, gain, store)

    def convolve(index):
        cols = pl.ds(pl.multiple_of(index * width, LANES), width)
        filt = jnp.dot(fwd[...], taps[index], preferred_element_type=jnp.float32)
        sr, si = spec[:block, cols], spec[block:, cols]
        fr, fi = filt[:block], filt[block:]
        prod_r = (sr * fr - si * fi).astype(jnp.bfloat16)
        prod_i = (sr * fi + si * fr).astype(jnp.bfloat16)
        conv[:, cols] = jnp.dot(
            inv[:, :block], prod_r, preferred_element_type=jnp.float32
        ) + jnp.dot(inv[:, block:], prod_i, preferred_element_type=jnp.float32)

    make_taps(0)

    @pl.loop(0, chunks - 1)
    def _(index):
        convolve(index)
        make_taps(index + 1)

    convolve(chunks - 1)

    def out_copies(index):
        cols = pl.ds(pl.multiple_of(index * width, LANES), width)
        target = pl.ds(pl.multiple_of(my_cols + index * width, LANES), width)
        local = pltpu.make_async_copy(
            outb.at[my_rows, cols], out_hbm.at[:, target], out_sem.at[0, index]
        )
        remote = pltpu.make_async_remote_copy(
            src_ref=outb.at[mate_rows, cols], dst_ref=out_hbm.at[:, target],
            send_sem=out_sem.at[1, index], recv_sem=out_sem.at[2, index],
            device_id={"ctx": mate}, device_id_type=MESH,
        )
        return local, remote

    @pl.loop(0, chunks)
    def _(index):
        for earlier in range(pairs - 1):

            @pl.when(earlier < pos)
            def _():
                state_copy(index, pos, earlier).wait_recv()

        @pl.when(pos > 0)
        def _():
            @pl.loop(0, groups, unroll=True)
            def _(inner):
                group = index * groups + inner
                cols = pl.ds(pl.multiple_of(group * LANES, LANES), LANES)
                decay, gain = group_params(group)
                across = jnp.exp(-float(block) * decay)
                total = jnp.zeros((modes, LANES), jnp.float32)
                for earlier in range(pairs - 1):
                    total = jnp.where(
                        earlier < pos,
                        total * across + staten[earlier, :, cols].astype(jnp.float32),
                        total,
                    )
                start = total * gain * jnp.exp(-decay)

                direct = group_skip(group)

                def store(row, sums):
                    rows = pl.ds(row, 16)
                    outb[rows, cols] = (
                        conv[rows, cols] + sums + direct * mixf[rows, cols].astype(jnp.float32)
                    ).astype(jnp.bfloat16)

                exp_sums(decay, start, store)

        @pl.when(pos == 0)
        def _():
            @pl.loop(0, groups, unroll=True)
            def _(inner):
                group = index * groups + inner
                cols = pl.ds(pl.multiple_of(group * LANES, LANES), LANES)
                outb[:, cols] = (
                    conv[:, cols] + group_skip(group) * mixf[:, cols].astype(jnp.float32)
                ).astype(jnp.bfloat16)

        local, remote = out_copies(index)
        local.start()
        remote.start()

    @pl.when(owns)
    def _():
        for step in range(1, dp_size):
            target = (dp + step) % dp_size
            par_copy(slot, target, step - 1).wait_send()
            skp_copy(slot, target, step - 1).wait_send()

    send_mix.wait_send()
    for index in range(chunks):
        for later in range(1, pairs):

            @pl.when(pos < later)
            def _():
                state_copy(index, later, pos).wait_send()

        local, remote = out_copies(index)
        local.wait()
        remote.wait()


def body(queries, keys, values, rates, residues, skip):
    tokens, channels = queries.shape[1:]
    shard, modes = rates.shape
    ctx_size = lax.axis_size("ctx")
    dp_size = lax.axis_size("dp")
    pairs = ctx_size // 2
    half = channels // 2
    block = 2 * tokens
    width = min(512, half)
    chunks = half // width
    forward, inverse = transforms(block)
    hbm_spec = pl.BlockSpec(memory_space=pltpu.HBM)
    bf16, f32 = jnp.bfloat16, jnp.float32
    slots = max(pairs - 1, 1)
    dma = pltpu.SemaphoreType.DMA
    sizes = (tokens, half, shard, modes, ctx_size, dp_size, width)
    mixed_out = pl.pallas_call(
        functools.partial(kernel, sizes),
        out_shape=jax.ShapeDtypeStruct((tokens, channels), bf16),
        in_specs=[hbm_spec] * 7,
        out_specs=hbm_spec,
        scratch_shapes=[
            pltpu.VMEM((modes, shard), f32),
            pltpu.VMEM((modes, shard), f32),
            pltpu.VMEM((tokens, channels), bf16),
            pltpu.VMEM((tokens, channels), bf16),
            pltpu.VMEM((tokens, half), bf16),
            pltpu.VMEM((block, half), bf16),
            pltpu.VMEM((block, half), bf16),
            pltpu.VMEM((dp_size // 2, 2, modes, shard), bf16),
            pltpu.VMEM((dp_size // 2, 1, shard), f32),
            pltpu.VMEM((chunks, block, width), bf16),
            pltpu.VMEM((2 * block, half), f32),
            pltpu.VMEM((block, half), f32),
            pltpu.VMEM((2 * block, block), bf16),
            pltpu.VMEM((block, 2 * block), bf16),
            pltpu.VMEM((modes, LANES), f32),
            pltpu.VMEM((modes, half), bf16),
            pltpu.VMEM((slots, modes, half), bf16),
            dma((8,)),
            dma((2,)),
            dma((dp_size - 1,)),
            dma((dp_size // 2,)),
            dma((dp_size - 1,)),
            dma((dp_size // 2,)),
            dma((pairs, chunks)),
            dma((slots, chunks)),
            dma((3, chunks)),
        ],
        compiler_params=pltpu.CompilerParams(
            collective_id=0, has_side_effects=True, vmem_limit_bytes=60 * 2**20
        ),
    )(
        keys[0], values[0], rates.T, residues.T, skip[None, :],
        jnp.asarray(forward), jnp.asarray(inverse),
    )
    return (queries.astype(f32) * mixed_out[None].astype(f32)).astype(bf16)


def solution(mesh):
    in_specs = (
        P("dp", "ctx", "tp"),
        P("dp", "ctx", "tp"),
        P("dp", "ctx", "tp"),
        P(("tp", "dp"), None),
        P(("tp", "dp"), None),
        P(("tp", "dp")),
    )
    out_specs = P("dp", "ctx", "tp")
    return jax.shard_map(body, mesh=mesh, in_specs=in_specs, out_specs=out_specs, check_vma=False)
```
